256 devices in a mesh: seq: 64 (over y_hi, x, z), chan: 4 (over y_lo, core).
Axes of the slice: x: 4, y: 4 (y_hi: 2, y_lo: 2; y = y_hi * 2 + y_lo), z: 8, core: 2. Of those that a mesh axis runs over, the one named last changes fastest.
Arguments:
- inputs: bfloat16 [16384, 2048], P('seq', 'chan'), may hold values from -6 to 6
- weights: bfloat16 [4, 2048, 2048], P(None, None, 'chan'), may hold values from -0.125 to 0.125
- filters: float32 [4, 16384], P(None, 'seq'), may hold values from -0.046875 to 0.046875
Outputs:
- output: bfloat16 [16384, 2048], P('seq', 'chan')
The draws below stay inside these ranges and needn't reach their ends.
All inputs are finite; a program needn't handle non-finite values.
Results may differ from the reference program's by a relative error of at most 0.0049.
Values may be sent and summed in bfloat16 or wider, within the bound.
A program may use at most 64 MiB of HBM per device.

```python
import jax
import jax.numpy as jnp
from jax import lax

D = 2048
K = 4
L = 16384


def steps_of(rng, shape, pieces, low, top_value):
    gain, own = 1.0, jax.random.fold_in(rng, 6)
    for axis_at, shards_of in pieces:
        steps = jnp.exp(jax.random.uniform(jax.random.fold_in(own, axis_at), (shards_of,), jnp.float32, low / len(pieces), top_value / len(pieces)))
        gain = gain * jnp.repeat(steps, shape[axis_at] // shards_of).reshape([-1 if axis == axis_at else 1 for axis in range(len(shape))])
    return gain


def noise(key, extent, spread, most, split=(), held_as=jnp.bfloat16):
    drawn = spread * jax.random.normal(key, extent, jnp.float32)
    if split:
        drawn = drawn * steps_of(key, extent, split, -0.22, 0.18)
    return jnp.clip(drawn, -most, most).astype(held_as)


def setup_inputs(seed: int = 0) -> dict:
    key_list = jax.random.split(jax.random.key(seed), 4)
    inputs = noise(key_list[0], (L, D), 1.0, 6.0, ((0, 64), (1, 4)))
    weights = noise(key_list[1], (K, D, D), D ** -0.5, 0.125, ((2, 4),))
    filters = noise(key_list[2], (K, L), L ** -0.5, 0.046875, ((1, 64),), jnp.float32)
    return dict(inputs=inputs, weights=weights, filters=filters)


def reference(inputs, weights, filters):
    length = inputs.shape[0]
    total = 2 * length

    def add_filter(summed, pair):
        weight, filter_row = pair
        projected = jnp.dot(inputs, weight, preferred_element_type=jnp.float32).astype(jnp.bfloat16)
        projected = lax.optimization_barrier(projected).astype(jnp.float32)
        spectrum = jnp.fft.rfft(projected, n=total, axis=0) * jnp.fft.rfft(filter_row, n=total)[:, None]
        convolved = jnp.fft.irfft(spectrum, n=total, axis=0)[:length]
        return summed + convolved.astype(summed.dtype), None

    start = jnp.zeros(inputs.shape, jnp.float32)
    summed, unused = lax.scan(add_filter, start, (weights, filters))
    return summed.astype(jnp.bfloat16)
```

```python
import functools

import jax
import jax.numpy as jnp
from jax import lax
from jax.experimental import pallas as pl
from jax.experimental.pallas import tpu as pltpu
from jax.sharding import PartitionSpec as P

MESH = pl.DeviceIdType.MESH
SEQ = 64
CHAN = 4
K = 4
TOK = 256
FEAT = 512
HALF = 128
SHARE = FEAT // SEQ
LAGS = 8
PARTS = 4


def peer(s, o):
    yh, x, z = s // 32, (s // 8) % 4, s % 8
    oy, ox, oz = o // 32, o % 4, (o // 4) % 8
    return ((yh + oy) % 2) * 32 + ((x + ox) % 4) * 8 + (z + oz) % 8


def wait_bytes(ref, sem):
    pltpu.make_async_copy(ref, ref, sem).wait()


def toeplitz(flt, table):
    row = lax.broadcasted_iota(jnp.int32, (HALF, HALF), 0)
    col = lax.broadcasted_iota(jnp.int32, (HALF, HALF), 1)
    same = col >= row

    def turned(line):
        return pltpu.roll(
            jnp.broadcast_to(line, (HALF, HALF)), 0, axis=1, stride=1, stride_axis=0
        )

    for k in range(K):
        table[k, 0] = jnp.zeros((HALF, HALF), jnp.bfloat16)

        def step(m, before):
            first = turned(flt[m, pl.ds(k, 1), :])
            table[k, 2 * m + 1] = jnp.where(same, first, before).astype(jnp.bfloat16)
            second = turned(flt[m, pl.ds(K + k, 1), :])
            table[k, 2 * m + 2] = jnp.where(same, second, first).astype(jnp.bfloat16)
            return second

        lax.fori_loop(0, SEQ, step, jnp.zeros((HALF, HALF), jnp.float32))


def load_blocks(got, k, even, odd):
    v = got[k].astype(jnp.float32)
    a = jnp.concatenate([v[:, :SHARE, :], v[:, SHARE:, :]], axis=2)
    a = a.reshape(SEQ * SHARE, TOK)
    even[pl.ds(64, 512), :] = a.astype(jnp.bfloat16)
    zero = jnp.zeros((SHARE, TOK), jnp.float32)
    odd[pl.ds(64, 528), :] = jnp.concatenate([zero, a, zero], axis=0).astype(jnp.bfloat16)


def conv_lags(table, even, odd, acc, k, group, fresh):
    low = 64 * group
    rows = 512 - low
    lhs, rhs = [], []
    for jj in range(LAGS):
        at = 64 - 8 * jj
        lhs.append(even[at : at + rows, :] if jj % 2 == 0 else odd[at + 8 : at + 8 + rows, :])
        n = 2 * (LAGS * group + jj) + 1
        rhs.append(jnp.concatenate([table[k, n], table[k, n + 1]], axis=1))
        rhs.append(jnp.concatenate([table[k, n - 1], table[k, n]], axis=1))
    part = jnp.dot(
        jnp.concatenate(lhs, axis=1),
        jnp.concatenate(rhs, axis=0),
        preferred_element_type=jnp.float32,
    )
    if fresh:
        acc[low:, :] = part
    else:
        acc[low:, :] += part


def kernel(
    x_ref, w_hbm, f_ref, o_ref,
    xs, w, fsrc, flt, out_p, got, table, even, odd, acc, out_y, got_y,
    w_sem, xs_send, xs_recv, f_send, f_recv, p_send, p_recv, y_send, y_recv,
):
    s, c = lax.axis_index("seq"), lax.axis_index("chan")
    mate = c + 1 - 2 * (c % 2)
    across = (c + 2) % 4

    bar = pltpu.get_barrier_semaphore()
    for i in range(1, CHAN):
        pl.semaphore_signal(bar, inc=1, device_id=(s, (c + i) % CHAN), device_id_type=MESH)

    @pl.loop(1, SEQ)
    def _(o):
        pl.semaphore_signal(bar, inc=1, device_id=(peer(s, o), c), device_id_type=MESH)

    for k in range(K):
        pltpu.make_async_copy(w_hbm.at[k], w.at[k], w_sem.at[k]).start()
    f = f_ref[...]
    fsrc[...] = jnp.concatenate([f[:, :HALF], f[:, HALF:]], axis=0)
    xs[pl.ds(c, 1)] = x_ref[...][None]
    flt[pl.ds(s, 1)] = fsrc[...][None]
    even[0:64, :] = jnp.zeros((64, TOK), jnp.bfloat16)
    odd[0:64, :] = jnp.zeros((64, TOK), jnp.bfloat16)
    pl.semaphore_wait(bar, SEQ - 1 + CHAN - 1)

    rows = TOK // PARTS

    def x_copy(owner, part, to, kind):
        at = xs.at[owner, pl.ds(part * rows, rows)]
        return pltpu.make_async_remote_copy(
            at, at, xs_send.at[kind, part], xs_recv.at[kind, part],
            device_id=(s, to), device_id_type=MESH,
        )

    for part in range(PARTS):
        x_copy(c, part, across, 0).start()
    for part in range(PARTS):
        x_copy(c, part, mate, 1).start()

    @pl.loop(1, SEQ)
    def _(o):
        pltpu.make_async_remote_copy(
            fsrc, flt.at[s], f_send, f_recv, device_id=(peer(s, o), c), device_id_type=MESH
        ).start()

    for part in range(PARTS):
        x_copy(across, part, across, 0).wait_recv()
        x_copy(across, part, mate, 2).start()
    for part in range(PARTS):
        x_copy(mate, part, mate, 1).wait_recv()
    for part in range(PARTS):
        x_copy((across + mate - c + 4) % 4, part, mate, 2).wait_recv()

    for k in range(K):
        pltpu.make_async_copy(w_hbm.at[k], w.at[k], w_sem.at[k]).wait()
        p = None
        for i in range(CHAN):
            d = jnp.dot(
                xs[i], w[k, i * FEAT : (i + 1) * FEAT, :], preferred_element_type=jnp.float32
            )
            p = d if p is None else p + d
        t = p.T.reshape(SEQ, SHARE, TOK)
        out_p[k] = jnp.concatenate([t[:, :, :HALF], t[:, :, HALF:]], axis=1).astype(jnp.bfloat16)

        @pl.loop(1, SEQ)
        def _(o):
            to = peer(s, o)
            pltpu.make_async_remote_copy(
                out_p.at[k, to], got.at[k, s], p_send.at[k], p_recv.at[k],
                device_id=(to, c), device_id_type=MESH,
            ).start()

        got[k, pl.ds(s, 1)] = out_p[k, pl.ds(s, 1)]

    wait_bytes(flt.at[pl.ds(0, SEQ - 1)], f_recv)
    toeplitz(flt, table)

    for k in range(K):
        wait_bytes(got.at[k, pl.ds(0, SEQ - 1)], p_recv.at[k])
        load_blocks(got, k, even, odd)
        for group in range(SEQ // LAGS):
            conv_lags(table, even, odd, acc, k, group, k == 0 and group == 0)

    y = acc[...].reshape(SEQ, SHARE, TOK)
    out_y[...] = jnp.concatenate([y[:, :, :HALF], y[:, :, HALF:]], axis=1).astype(jnp.bfloat16)

    @pl.loop(1, SEQ)
    def _(o):
        to = peer(s, o)
        pltpu.make_async_remote_copy(
            out_y.at[to], got_y.at[s], y_send, y_recv, device_id=(to, c), device_id_type=MESH
        ).start()

    got_y[pl.ds(s, 1)] = out_y[pl.ds(s, 1)]
    for part in range(PARTS):
        x_copy(c, part, across, 0).wait_send()
        x_copy(c, part, mate, 1).wait_send()
        x_copy(across, part, mate, 2).wait_send()
    wait_bytes(flt.at[pl.ds(0, SEQ - 1)], f_send)
    for k in range(K):
        wait_bytes(out_p.at[k, pl.ds(0, SEQ - 1)], p_send.at[k])

    wait_bytes(got_y.at[pl.ds(0, SEQ - 1)], y_recv)
    r = got_y[...].astype(jnp.float32)
    for half in range(2):
        block = r[:, half * SHARE : (half + 1) * SHARE, :].reshape(FEAT, HALF)
        o_ref[half * HALF : (half + 1) * HALF, :] = block.T.astype(jnp.bfloat16)
    wait_bytes(out_y.at[pl.ds(0, SEQ - 1)], y_send)


def local(inputs, weights, filters):
    bf16, f32 = jnp.bfloat16, jnp.float32
    vmem = pl.BlockSpec(memory_space=pltpu.VMEM)
    dma = pltpu.SemaphoreType.DMA
    return pl.pallas_call(
        kernel,
        out_shape=jax.ShapeDtypeStruct((TOK, FEAT), bf16),
        in_specs=[vmem, pl.BlockSpec(memory_space=pl.ANY), vmem],
        out_specs=vmem,
        scratch_shapes=[
            pltpu.VMEM((CHAN, TOK, FEAT), bf16),
            pltpu.VMEM((K, CHAN * FEAT, FEAT), bf16),
            pltpu.VMEM((8, HALF), f32),
            pltpu.VMEM((SEQ, 8, HALF), f32),
            pltpu.VMEM((K, SEQ, 16, HALF), bf16),
            pltpu.VMEM((K, SEQ, 16, HALF), bf16),
            pltpu.VMEM((K, 2 * SEQ + 1, HALF, HALF), bf16),
            pltpu.VMEM((576, TOK), bf16),
            pltpu.VMEM((592, TOK), bf16),
            pltpu.VMEM((512, TOK), f32),
            pltpu.VMEM((SEQ, 16, HALF), bf16),
            pltpu.VMEM((SEQ, 16, HALF), bf16),
            dma((K,)),
            dma((3, PARTS)),
            dma((3, PARTS)),
            dma,
            dma,
            dma((K,)),
            dma((K,)),
            dma,
            dma,
        ],
        compiler_params=pltpu.CompilerParams(
            collective_id=0, has_side_effects=True, vmem_limit_bytes=56 << 20
        ),
        cost_estimate=pl.CostEstimate(
            flops=11 * 10**9, bytes_accessed=10**7, transcendentals=0
        ),
    )(inputs, weights, filters)


def solution(mesh):
    in_specs = (P("seq", "chan"), P(None, None, "chan"), P(None, "seq"))
    out_specs = P("seq", "chan")
    return jax.shard_map(local, mesh=mesh, in_specs=in_specs, out_specs=out_specs, check_vma=False)
```

```python
import functools

import jax
import jax.numpy as jnp
from jax import lax
from jax.experimental import pallas as pl
from jax.experimental.pallas import tpu as pltpu
from jax.sharding import PartitionSpec as P

MESH = pl.DeviceIdType.MESH
SEQ = 64
CHAN = 4
K = 4
TOK = 256
FEAT = 512
HALF = 128
SHARE = FEAT // SEQ
LAGS = 8
BLOCKS = 8
PARTS = 4


def peer(s, c, o):
    i, r = (SEQ - o) // 8, (SEQ - o) % 8
    h = (i + 1) // 2
    oz = h + (1 - i % 2) * (8 - 2 * h)
    oz = oz + (c % 2) * (8 - 2 * oz)
    yh, x, z = s // 32, (s // 8) % 4, s % 8
    return ((yh + r // 4) % 2) * 32 + ((x + r) % 4) * 8 + (z + oz) % 8


def wait_bytes(ref, sem):
    pltpu.make_async_copy(ref, ref, sem).wait()


def toeplitz(flt, table):
    row = lax.broadcasted_iota(jnp.int32, (16, HALF), 0)
    col = lax.broadcasted_iota(jnp.int32, (16, HALF), 1)

    def turned(line):
        wide = jnp.broadcast_to(line, (16, HALF))
        return pltpu.roll(wide, 0, axis=1, stride=1, stride_axis=0).astype(jnp.bfloat16)

    for k in range(K):
        table[k, 0] = jnp.zeros((HALF, HALF), jnp.bfloat16)

    def step(m0, carry):
        for k in range(K):
            last = flt[jnp.maximum(m0 * BLOCKS - 1, 0), pl.ds(K + k, 1), :]
            base = [turned(jnp.where(m0 == 0, 0.0, last))]
            for m in range(BLOCKS):
                for q in range(2):
                    base.append(turned(flt[m0 * BLOCKS + m, pl.ds(q * K + k, 1), :]))
            for i in range(HALF // 16):
                moved = base if i == 0 else [pltpu.roll(b, 16 * i, axis=1) for b in base]
                for n in range(2 * BLOCKS):
                    table[k, 2 * BLOCKS * m0 + n + 1, 16 * i : 16 * (i + 1), :] = jnp.where(
                        col >= row + 16 * i, moved[n + 1], moved[n]
                    )
        return carry

    lax.fori_loop(0, SEQ // BLOCKS, step, 0)


def load_blocks(got, chunk, even, odd):
    v = got[chunk].astype(jnp.float32)
    zero = jnp.zeros((SHARE, HALF), jnp.float32)
    for kk in range(2):
        a = v[:, kk * SHARE : (kk + 1) * SHARE, :].reshape(SEQ * SHARE, HALF)
        even[kk, 64:576, :] = a.astype(jnp.bfloat16)
        odd[kk, 64:592, :] = jnp.concatenate([zero, a, zero], axis=0).astype(jnp.bfloat16)


def conv_lags(table, even, odd, acc, chunk, group):
    half, pair = chunk // 2, chunk % 2
    low = 64 * group
    rows = 512 - low
    lhs, rhs = [], []
    for kk in range(2):
        for jj in range(LAGS):
            at = 64 - 8 * jj
            if jj % 2 == 0:
                lhs.append(even[kk, at : at + rows, :])
            else:
                lhs.append(odd[kk, at + 8 : at + 8 + rows, :])
            n = 2 * (LAGS * group + jj) + 1 - half
            k = 2 * pair + kk
            rhs.append(jnp.concatenate([table[k, n], table[k, n + 1]], axis=1))
    part = jnp.dot(
        jnp.concatenate(lhs, axis=1),
        jnp.concatenate(rhs, axis=0),
        preferred_element_type=jnp.float32,
    )
    if chunk == 0 and group == 0:
        acc[low:, :] = part
    else:
        acc[low:, :] += part


def kernel(
    x_ref, w_hbm, f_ref, o_ref,
    xs, w, fsrc, flt, part_p, out_p, got, table, even, odd, acc, out_y, got_y,
    w_sem, xs_send, xs_recv, f_send, f_recv, p_send, p_recv, y_send, y_recv,
):
    s, c = lax.axis_index("seq"), lax.axis_index("chan")
    mate = c + 1 - 2 * (c % 2)
    across = (c + 2) % 4
    diag = (mate + 2) % 4

    bar = pltpu.get_barrier_semaphore()
    for i in range(1, CHAN):
        pl.semaphore_signal(bar, inc=1, device_id=(s, (c + i) % CHAN), device_id_type=MESH)

    @pl.loop(1, SEQ)
    def _(o):
        pl.semaphore_signal(bar, inc=1, device_id=(peer(s, c, o), c), device_id_type=MESH)

    for k in range(K):
        pltpu.make_async_copy(w_hbm.at[k], w.at[k], w_sem.at[k]).start()
    f = f_ref[...]
    fsrc[...] = jnp.concatenate([f[:, :HALF], f[:, HALF:]], axis=0)
    xs[pl.ds(c, 1)] = x_ref[...][None]
    flt[pl.ds(s, 1)] = fsrc[...][None]
    for kk in range(2):
        even[kk, 0:64, :] = jnp.zeros((64, HALF), jnp.bfloat16)
        odd[kk, 0:64, :] = jnp.zeros((64, HALF), jnp.bfloat16)
    pl.semaphore_wait(bar, SEQ - 1 + CHAN - 1)

    rows = TOK // PARTS

    def x_copy(owner, part, to, kind):
        at = xs.at[owner, pl.ds(part * rows, rows)]
        return pltpu.make_async_remote_copy(
            at, at, xs_send.at[kind, part], xs_recv.at[kind, part],
            device_id=(s, to), device_id_type=MESH,
        )

    for part in range(PARTS):
        x_copy(c, part, across, 0).start()
    for part in range(PARTS):
        x_copy(c, part, mate, 1).start()

    @pl.loop(1, SEQ)
    def _(o):
        pltpu.make_async_remote_copy(
            fsrc, flt.at[s], f_send, f_recv, device_id=(peer(s, c, o), c), device_id_type=MESH
        ).start()

    def pass_on(part):
        x_copy(across, part, across, 0).wait_recv()
        x_copy(across, part, mate, 2).start()

    def project(owner, k, low, high):
        return jnp.dot(
            xs[owner, low:high, :],
            w[k, pl.ds(pl.multiple_of(owner * FEAT, FEAT), FEAT), :],
            preferred_element_type=jnp.float32,
        )

    for k in range(K):
        pltpu.make_async_copy(w_hbm.at[k], w.at[k], w_sem.at[k]).wait()
        part_p[k] = project(c, k, 0, TOK)
    pass_on(0)
    for part in range(PARTS):
        x_copy(mate, part, mate, 1).wait_recv()
    pass_on(1)
    for k in range(K):
        part_p[k] += project(mate, k, 0, TOK)

    for chunk in range(4):
        half, pair = chunk // 2, chunk % 2
        if chunk == 1:
            pass_on(2)
            pass_on(3)
        if pair == 0:
            x_copy(diag, 2 * half, mate, 2).wait_recv()
            x_copy(diag, 2 * half + 1, mate, 2).wait_recv()
        low, high = half * HALF, (half + 1) * HALF
        turned = []
        for k in (2 * pair, 2 * pair + 1):
            p = part_p[k, low:high, :] + project(across, k, low, high) + project(diag, k, low, high)
            turned.append(p.T.reshape(SEQ, SHARE, HALF))
        out_p[chunk] = jnp.concatenate(turned, axis=1).astype(jnp.bfloat16)

        @pl.loop(1, SEQ)
        def _(o):
            to = peer(s, c, o)
            pltpu.make_async_remote_copy(
                out_p.at[chunk, to], got.at[chunk, s], p_send.at[chunk], p_recv.at[chunk],
                device_id=(to, c), device_id_type=MESH,
            ).start()

        got[chunk, pl.ds(s, 1)] = out_p[chunk, pl.ds(s, 1)]

    wait_bytes(flt.at[pl.ds(0, SEQ - 1)], f_recv)
    toeplitz(flt, table)

    for chunk in range(4):
        wait_bytes(got.at[chunk, pl.ds(0, SEQ - 1)], p_recv.at[chunk])
        load_blocks(got, chunk, even, odd)
        for group in range(SEQ // LAGS):
            conv_lags(table, even, odd, acc, chunk, group)

    y = acc[...].reshape(SEQ, SHARE, TOK)
    out_y[...] = jnp.concatenate([y[:, :, :HALF], y[:, :, HALF:]], axis=1).astype(jnp.bfloat16)

    @pl.loop(1, SEQ)
    def _(o):
        to = peer(s, c, o)
        pltpu.make_async_remote_copy(
            out_y.at[to], got_y.at[s], y_send, y_recv, device_id=(to, c), device_id_type=MESH
        ).start()

    got_y[pl.ds(s, 1)] = out_y[pl.ds(s, 1)]
    for part in range(PARTS):
        x_copy(c, part, across, 0).wait_send()
        x_copy(c, part, mate, 1).wait_send()
        x_copy(across, part, mate, 2).wait_send()
    wait_bytes(flt.at[pl.ds(0, SEQ - 1)], f_send)
    for k in range(K):
        wait_bytes(out_p.at[k, pl.ds(0, SEQ - 1)], p_send.at[k])

    wait_bytes(got_y.at[pl.ds(0, SEQ - 1)], y_recv)
    r = got_y[...].astype(jnp.float32)
    for half in range(2):
        block = r[:, half * SHARE : (half + 1) * SHARE, :].reshape(FEAT, HALF)
        o_ref[half * HALF : (half + 1) * HALF, :] = block.T.astype(jnp.bfloat16)
    wait_bytes(out_y.at[pl.ds(0, SEQ - 1)], y_send)


def local(inputs, weights, filters):
    bf16, f32 = jnp.bfloat16, jnp.float32
    vmem = pl.BlockSpec(memory_space=pltpu.VMEM)
    dma = pltpu.SemaphoreType.DMA
    return pl.pallas_call(
        kernel,
        out_shape=jax.ShapeDtypeStruct((TOK, FEAT), bf16),
        in_specs=[vmem, pl.BlockSpec(memory_space=pl.ANY), vmem],
        out_specs=vmem,
        scratch_shapes=[
            pltpu.VMEM((CHAN, TOK, FEAT), bf16),
            pltpu.VMEM((K, CHAN * FEAT, FEAT), bf16),
            pltpu.VMEM((8, HALF), f32),
            pltpu.VMEM((SEQ, 8, HALF), f32),
            pltpu.VMEM((K, TOK, FEAT), f32),
            pltpu.VMEM((K, SEQ, 16, HALF), bf16),
            pltpu.VMEM((K, SEQ, 16, HALF), bf16),
            pltpu.VMEM((K, 2 * SEQ + 1, HALF, HALF), bf16),
            pltpu.VMEM((2, 576, HALF), bf16),
            pltpu.VMEM((2, 592, HALF), bf16),
            pltpu.VMEM((512, TOK), f32),
            pltpu.VMEM((SEQ, 16, HALF), bf16),
            pltpu.VMEM((SEQ, 16, HALF), bf16),
            dma((K,)),
            dma((3, PARTS)),
            dma((3, PARTS)),
            dma,
            dma,
            dma((K,)),
            dma((K,)),
            dma,
            dma,
        ],
        compiler_params=pltpu.CompilerParams(
            collective_id=0, has_side_effects=True, vmem_limit_bytes=56 << 20
        ),
        cost_estimate=pl.CostEstimate(
            flops=11 * 10**9, bytes_accessed=10**7, transcendentals=0
        ),
    )(inputs, weights, filters)


def solution(mesh):
    in_specs = (P("seq", "chan"), P(None, None, "chan"), P(None, "seq"))
    out_specs = P("seq", "chan")
    return jax.shard_map(local, mesh=mesh, in_specs=in_specs, out_specs=out_specs, check_vma=False)
```

```python
import functools

import jax
import jax.numpy as jnp
from jax import lax
from jax.experimental import pallas as pl
from jax.experimental.pallas import tpu as pltpu
from jax.sharding import PartitionSpec as P

MESH = pl.DeviceIdType.MESH
SEQ = 64
CHAN = 4
K = 4
TOK = 256
FEAT = 512
HALF = 128
SHARE = FEAT // SEQ
LAGS = 8
BLOCKS = 8
PARTS = 4


def peer(s, c, o):
    i, r = (SEQ - o) // 8, (SEQ - o) % 8
    h = (i + 1) // 2
    oz = h + (1 - i % 2) * (8 - 2 * h)
    oz = oz + (c % 2) * (8 - 2 * oz)
    yh, x, z = s // 32, (s // 8) % 4, s % 8
    return ((yh + r // 4) % 2) * 32 + ((x + r) % 4) * 8 + (z + oz) % 8


def wait_bytes(ref, sem):
    pltpu.make_async_copy(ref, ref, sem).wait()


def toeplitz(flt, table):
    row = lax.broadcasted_iota(jnp.int32, (16, HALF), 0)
    col = lax.broadcasted_iota(jnp.int32, (16, HALF), 1)

    def turned(line):
        wide = jnp.broadcast_to(line, (16, HALF))
        return pltpu.roll(wide, 0, axis=1, stride=1, stride_axis=0).astype(jnp.bfloat16)

    for k in range(K):
        table[k, 0] = jnp.zeros((HALF, HALF), jnp.bfloat16)

    def step(m0, carry):
        for k in range(K):
            last = flt[jnp.maximum(m0 * BLOCKS - 1, 0), pl.ds(K + k, 1), :]
            base = [turned(jnp.where(m0 == 0, 0.0, last))]
            for m in range(BLOCKS):
                for q in range(2):
                    base.append(turned(flt[m0 * BLOCKS + m, pl.ds(q * K + k, 1), :]))
            for i in range(HALF // 16):
                moved = base if i == 0 else [pltpu.roll(b, 16 * i, axis=1) for b in base]
                for n in range(2 * BLOCKS):
                    table[k, 2 * BLOCKS * m0 + n + 1, 16 * i : 16 * (i + 1), :] = jnp.where(
                        col >= row + 16 * i, moved[n + 1], moved[n]
                    )
        return carry

    lax.fori_loop(0, SEQ // BLOCKS, step, 0)


def load_blocks(got, chunk, even, odd):
    v = got[chunk].astype(jnp.float32)
    zero = jnp.zeros((SHARE, HALF), jnp.float32)
    for kk in range(2):
        a = v[:, kk * SHARE : (kk + 1) * SHARE, :].reshape(SEQ * SHARE, HALF)
        even[kk, 64:576, :] = a.astype(jnp.bfloat16)
        odd[kk, 64:592, :] = jnp.concatenate([zero, a, zero], axis=0).astype(jnp.bfloat16)


def conv_lags(table, even, odd, acc, chunk, group):
    half, pair = chunk // 2, chunk % 2
    low = 64 * group
    rows = 512 - low
    lhs, rhs = [], []
    for kk in range(2):
        for jj in range(LAGS):
            at = 64 - 8 * jj
            if jj % 2 == 0:
                lhs.append(even[kk, at : at + rows, :])
            else:
                lhs.append(odd[kk, at + 8 : at + 8 + rows, :])
            n = 2 * (LAGS * group + jj) + 1 - half
            k = 2 * pair + kk
            rhs.append(jnp.concatenate([table[k, n], table[k, n + 1]], axis=1))
    part = jnp.dot(
        jnp.concatenate(lhs, axis=1),
        jnp.concatenate(rhs, axis=0),
        preferred_element_type=jnp.float32,
    )
    if chunk == 0 and group == 0:
        acc[low:, :] = part
    else:
        acc[low:, :] += part


def kernel(
    x_hbm, w_hbm, f_hbm, got_y,
    xs, w, fsrc, flt, part_p, out_p, got, table, even, odd, acc, out_y,
    in_sem, w_sem, xs_send, xs_recv, f_send, f_recv, g_send, g_recv, p_send, p_recv, y_send, y_recv,
):
    s, c = lax.axis_index("seq"), lax.axis_index("chan")
    mate = c + 1 - 2 * (c % 2)
    across = (c + 2) % 4
    diag = (mate + 2) % 4

    bar = pltpu.get_barrier_semaphore()
    for i in range(1, CHAN):
        pl.semaphore_signal(bar, inc=1, device_id=(s, (c + i) % CHAN), device_id_type=MESH)

    @pl.loop(1, SEQ)
    def _(o):
        pl.semaphore_signal(bar, inc=1, device_id=((s + o) % SEQ, c), device_id_type=MESH)

    x_in = pltpu.make_async_copy(x_hbm, xs.at[c], in_sem.at[0])
    f_in = pltpu.make_async_copy(f_hbm, fsrc, in_sem.at[1])
    x_in.start()
    f_in.start()
    for k in range(K):
        pltpu.make_async_copy(w_hbm.at[k], w.at[k], w_sem.at[k]).start()
    for kk in range(2):
        even[kk, 0:64, :] = jnp.zeros((64, HALF), jnp.bfloat16)
        odd[kk, 0:64, :] = jnp.zeros((64, HALF), jnp.bfloat16)
    f_in.wait()
    f = fsrc[...]
    flt[pl.ds(s, 1)] = jnp.concatenate([f[:, :HALF], f[:, HALF:]], axis=0)[None]
    x_in.wait()
    pl.semaphore_wait(bar, SEQ - 1 + CHAN - 1)

    rows = TOK // PARTS

    def x_copy(owner, part, to, kind):
        at = xs.at[owner, pl.ds(part * rows, rows)]
        return pltpu.make_async_remote_copy(
            at, at, xs_send.at[kind, part], xs_recv.at[kind, part],
            device_id=(s, to), device_id_type=MESH,
        )

    for part in range(PARTS):
        x_copy(c, part, across, 0).start()
    for part in range(PARTS):
        x_copy(c, part, mate, 1).start()

    line, z = s // 8, s % 8

    def near_copy(i):
        return pltpu.make_async_remote_copy(
            flt.at[s], flt.at[s], f_send, f_recv,
            device_id=(line * 8 + (z + i) % 8, c), device_id_type=MESH,
        )

    def line_copy(i):
        block = flt.at[pl.ds(line * 8, 8)]
        return pltpu.make_async_remote_copy(
            block, block, g_send, g_recv,
            device_id=((line + i) % 8 * 8 + z, c), device_id_type=MESH,
        )

    for i in range(1, 8):
        near_copy(i).start()

    def pass_on(part):
        x_copy(across, part, across, 0).wait_recv()
        x_copy(across, part, mate, 2).start()

    def project(owner, k, low, high):
        return jnp.dot(
            xs[owner, low:high, :],
            w[k, pl.ds(pl.multiple_of(owner * FEAT, FEAT), FEAT), :],
            preferred_element_type=jnp.float32,
        )

    def own(k):
        pltpu.make_async_copy(w_hbm.at[k], w.at[k], w_sem.at[k]).wait()
        part_p[k] = project(c, k, 0, TOK)

    own(0)
    own(1)
    wait_bytes(flt.at[pl.ds(0, 7)], f_recv)
    for i in range(1, 8):
        line_copy(i).start()
    for part in range(PARTS):
        x_copy(mate, part, mate, 1).wait_recv()
    part_p[0] += project(mate, 0, 0, TOK)
    part_p[1] += project(mate, 1, 0, TOK)
    pass_on(0)
    own(2)
    pass_on(1)
    own(3)
    part_p[2] += project(mate, 2, 0, TOK)
    part_p[3] += project(mate, 3, 0, TOK)

    for chunk in range(4):
        half, pair = chunk // 2, chunk % 2
        if pair == 0:
            x_copy(diag, 2 * half, mate, 2).wait_recv()
            x_copy(diag, 2 * half + 1, mate, 2).wait_recv()
        if chunk == 0:
            pass_on(2)
        low, high = half * HALF, (half + 1) * HALF
        turned = []
        for k in (2 * pair, 2 * pair + 1):
            p = part_p[k, low:high, :] + project(across, k, low, high) + project(diag, k, low, high)
            turned.append(p.T.reshape(SEQ, SHARE, HALF))
        out_p[chunk] = jnp.concatenate(turned, axis=1).astype(jnp.bfloat16)
        if chunk == 0:
            pass_on(3)

        @pl.loop(1, SEQ)
        def _(o):
            to = peer(s, c, o)
            pltpu.make_async_remote_copy(
                out_p.at[chunk, to], got.at[chunk, s], p_send.at[chunk], p_recv.at[chunk],
                device_id=(to, c), device_id_type=MESH,
            ).start()

        got[chunk, pl.ds(s, 1)] = out_p[chunk, pl.ds(s, 1)]

    wait_bytes(flt.at[pl.ds(0, SEQ - 8)], g_recv)
    toeplitz(flt, table)

    for chunk in range(4):
        wait_bytes(got.at[chunk, pl.ds(0, SEQ - 1)], p_recv.at[chunk])
        load_blocks(got, chunk, even, odd)
        for group in range(SEQ // LAGS):
            conv_lags(table, even, odd, acc, chunk, group)
            if chunk == 3:
                y = acc[64 * group : 64 * (group + 1), :].reshape(LAGS, SHARE, TOK)
                y = jnp.concatenate([y[:, :, :HALF], y[:, :, HALF:]], axis=1)
                out_y[LAGS * group : LAGS * (group + 1)] = y.astype(jnp.bfloat16)

    @pl.loop(1, SEQ)
    def _(o):
        to = peer(s, c, o)
        pltpu.make_async_remote_copy(
            out_y.at[to], got_y.at[s], y_send, y_recv, device_id=(to, c), device_id_type=MESH
        ).start()

    got_y[pl.ds(s, 1)] = out_y[pl.ds(s, 1)]
    for part in range(PARTS):
        x_copy(c, part, across, 0).wait_send()
        x_copy(c, part, mate, 1).wait_send()
        x_copy(across, part, mate, 2).wait_send()
    wait_bytes(flt.at[pl.ds(0, 7)], f_send)
    wait_bytes(flt.at[pl.ds(0, SEQ - 8)], g_send)
    for k in range(K):
        wait_bytes(out_p.at[k, pl.ds(0, SEQ - 1)], p_send.at[k])

    wait_bytes(got_y.at[pl.ds(0, SEQ - 1)], y_recv)
    wait_bytes(out_y.at[pl.ds(0, SEQ - 1)], y_send)


def turn_back(y_ref, o_ref):
    r = y_ref[...].astype(jnp.float32)
    for half in range(2):
        block = r[:, half * SHARE : (half + 1) * SHARE, :].reshape(FEAT, HALF)
        o_ref[half * HALF : (half + 1) * HALF, :] = block.T.astype(jnp.bfloat16)


def local(inputs, weights, filters):
    bf16, f32 = jnp.bfloat16, jnp.float32
    vmem = pl.BlockSpec(memory_space=pltpu.VMEM)
    dma = pltpu.SemaphoreType.DMA
    y = pl.pallas_call(
        kernel,
        out_shape=jax.ShapeDtypeStruct((SEQ, 16, HALF), bf16),
        in_specs=[pl.BlockSpec(memory_space=pl.ANY)] * 3,
        out_specs=vmem,
        scratch_shapes=[
            pltpu.VMEM((CHAN, TOK, FEAT), bf16),
            pltpu.VMEM((K, CHAN * FEAT, FEAT), bf16),
            pltpu.VMEM((K, TOK), f32),
            pltpu.VMEM((SEQ, 8, HALF), f32),
            pltpu.VMEM((K, TOK, FEAT), f32),
            pltpu.VMEM((K, SEQ, 16, HALF), bf16),
            pltpu.VMEM((K, SEQ, 16, HALF), bf16),
            pltpu.VMEM((K, 2 * SEQ + 1, HALF, HALF), bf16),
            pltpu.VMEM((2, 576, HALF), bf16),
            pltpu.VMEM((2, 592, HALF), bf16),
            pltpu.VMEM((512, TOK), f32),
            pltpu.VMEM((SEQ, 16, HALF), bf16),
            dma((2,)),
            dma((K,)),
            dma((3, PARTS)),
            dma((3, PARTS)),
            dma,
            dma,
            dma,
            dma,
            dma((K,)),
            dma((K,)),
            dma,
            dma,
        ],
        compiler_params=pltpu.CompilerParams(
            collective_id=0, has_side_effects=True, vmem_limit_bytes=56 << 20
        ),
        cost_estimate=pl.CostEstimate(
            flops=11 * 10**9, bytes_accessed=10**7, transcendentals=0
        ),
    )(inputs, weights, filters)
    return pl.pallas_call(
        turn_back,
        out_shape=jax.ShapeDtypeStruct((TOK, FEAT), bf16),
        in_specs=[vmem],
        out_specs=vmem,
        cost_estimate=pl.CostEstimate(flops=0, bytes_accessed=2**19, transcendentals=0),
    )(y)


def solution(mesh):
    in_specs = (P("seq", "chan"), P(None, None, "chan"), P(None, "seq"))
    out_specs = P("seq", "chan")
    return jax.shard_map(local, mesh=mesh, in_specs=in_specs, out_specs=out_specs, check_vma=False)
```

```python
import functools

import jax
import jax.numpy as jnp
from jax import lax
from jax.experimental import pallas as pl
from jax.experimental.pallas import tpu as pltpu
from jax.sharding import PartitionSpec as P

MESH = pl.DeviceIdType.MESH
SEQ = 64
CHAN = 4
K = 4
TOK = 256
FEAT = 512
HALF = 128
SHARE = FEAT // SEQ
LAGS = 8
BLOCKS = 8
PARTS = 4


def for_peers(s, c, send):
    yh, x, z = s // 32, (s // 8) % 4, s % 8
    lines = [((yh + r // 4) % 2) * 32 + ((x + r) % 4) * 8 for r in range(8)]

    @pl.loop(0, 7)
    def _(j):
        i = 7 - j
        h = (i + 1) // 2
        oz = h + (1 - i % 2) * (8 - 2 * h)
        oz = oz + (c % 2) * (8 - 2 * oz)
        far = (z + oz) % 8
        for line in lines:
            send(line + far)

    for line in lines[1:]:
        send(line + z)


def wait_bytes(ref, sem):
    pltpu.make_async_copy(ref, ref, sem).wait()


def toeplitz(flt, table):
    row = lax.broadcasted_iota(jnp.int32, (16, HALF), 0)
    col = lax.broadcasted_iota(jnp.int32, (16, HALF), 1)

    def turned(line):
        wide = jnp.broadcast_to(line, (16, HALF))
        return pltpu.roll(wide, 0, axis=1, stride=1, stride_axis=0).astype(jnp.bfloat16)

    for k in range(K):
        table[k, 0] = jnp.zeros((HALF, HALF), jnp.bfloat16)

    def step(m0, carry):
        for k in range(K):
            last = flt[jnp.maximum(m0 * BLOCKS - 1, 0), pl.ds(K + k, 1), :]
            base = [turned(jnp.where(m0 == 0, 0.0, last))]
            for m in range(BLOCKS):
                for q in range(2):
                    base.append(turned(flt[m0 * BLOCKS + m, pl.ds(q * K + k, 1), :]))
            for i in range(HALF // 16):
                moved = base if i == 0 else [pltpu.roll(b, 16 * i, axis=1) for b in base]
                for n in range(2 * BLOCKS):
                    table[k, 2 * BLOCKS * m0 + n + 1, 16 * i : 16 * (i + 1), :] = jnp.where(
                        col >= row + 16 * i, moved[n + 1], moved[n]
                    )
        return carry

    lax.fori_loop(0, SEQ // BLOCKS, step, 0)


def load_blocks(got, chunk, even, odd):
    v = got[chunk].astype(jnp.float32)
    zero = jnp.zeros((SHARE, HALF), jnp.float32)
    for kk in range(2):
        a = v[:, kk * SHARE : (kk + 1) * SHARE, :].reshape(SEQ * SHARE, HALF)
        even[kk, 64:576, :] = a.astype(jnp.bfloat16)
        odd[kk, 64:592, :] = jnp.concatenate([zero, a, zero], axis=0).astype(jnp.bfloat16)


def conv_lags(table, even, odd, acc, chunk, group):
    half, pair = chunk // 2, chunk % 2
    low = 64 * group
    rows = 512 - low
    lhs, rhs = [], []
    for kk in range(2):
        for jj in range(LAGS):
            at = 64 - 8 * jj
            if jj % 2 == 0:
                lhs.append(even[kk, at : at + rows, :])
            else:
                lhs.append(odd[kk, at + 8 : at + 8 + rows, :])
            n = 2 * (LAGS * group + jj) + 1 - half
            k = 2 * pair + kk
            rhs.append(jnp.concatenate([table[k, n], table[k, n + 1]], axis=1))
    part = jnp.dot(
        jnp.concatenate(lhs, axis=1),
        jnp.concatenate(rhs, axis=0),
        preferred_element_type=jnp.float32,
    )
    if chunk == 0 and group == 0:
        acc[low:, :] = part
    else:
        acc[low:, :] += part


def kernel(
    x_hbm, w_hbm, f_hbm, got_y,
    xs, w, fsrc, flt, part_p, out_p, got, table, even, odd, acc, out_y,
    in_sem, w_sem, xs_send, xs_recv, f_send, f_recv, g_send, g_recv, p_send, p_recv, y_send, y_recv,
):
    s, c = lax.axis_index("seq"), lax.axis_index("chan")
    mate = c + 1 - 2 * (c % 2)
    across = (c + 2) % 4
    diag = (mate + 2) % 4

    bar = pltpu.get_barrier_semaphore()
    for i in range(1, CHAN):
        pl.semaphore_signal(bar, inc=1, device_id=(s, (c + i) % CHAN), device_id_type=MESH)

    for_peers(
        s, c, lambda to: pl.semaphore_signal(bar, inc=1, device_id=(to, c), device_id_type=MESH)
    )

    x_in = pltpu.make_async_copy(x_hbm, xs.at[c], in_sem.at[0])
    f_in = pltpu.make_async_copy(f_hbm, fsrc, in_sem.at[1])
    x_in.start()
    f_in.start()
    for k in range(K):
        pltpu.make_async_copy(w_hbm.at[k], w.at[k], w_sem.at[k]).start()
    for kk in range(2):
        even[kk, 0:64, :] = jnp.zeros((64, HALF), jnp.bfloat16)
        odd[kk, 0:64, :] = jnp.zeros((64, HALF), jnp.bfloat16)
    f_in.wait()
    f = fsrc[...]
    flt[pl.ds(s, 1)] = jnp.concatenate([f[:, :HALF], f[:, HALF:]], axis=0)[None]
    x_in.wait()
    pl.semaphore_wait(bar, SEQ - 1 + CHAN - 1)

    rows = TOK // PARTS

    def x_copy(owner, part, to, kind):
        at = xs.at[owner, pl.ds(part * rows, rows)]
        return pltpu.make_async_remote_copy(
            at, at, xs_send.at[kind, part], xs_recv.at[kind, part],
            device_id=(s, to), device_id_type=MESH,
        )

    for part in range(PARTS):
        x_copy(c, part, across, 0).start()
    for part in range(PARTS):
        x_copy(c, part, mate, 1).start()

    line, z = s // 8, s % 8

    def near_copy(i):
        return pltpu.make_async_remote_copy(
            flt.at[s], flt.at[s], f_send, f_recv,
            device_id=(line * 8 + (z + i) % 8, c), device_id_type=MESH,
        )

    def line_copy(i):
        block = flt.at[pl.ds(line * 8, 8)]
        return pltpu.make_async_remote_copy(
            block, block, g_send, g_recv,
            device_id=((line + i) % 8 * 8 + z, c), device_id_type=MESH,
        )

    for i in range(1, 8):
        near_copy(i).start()

    def pass_on(part):
        x_copy(across, part, across, 0).wait_recv()
        x_copy(across, part, mate, 2).start()

    def project(owner, k, low, high):
        return jnp.dot(
            xs[owner, low:high, :],
            w[k, pl.ds(pl.multiple_of(owner * FEAT, FEAT), FEAT), :],
            preferred_element_type=jnp.float32,
        )

    def own(k):
        pltpu.make_async_copy(w_hbm.at[k], w.at[k], w_sem.at[k]).wait()
        part_p[k] = project(c, k, 0, TOK)

    own(0)
    own(1)
    wait_bytes(flt.at[pl.ds(0, 7)], f_recv)
    for i in range(1, 8):
        line_copy(i).start()
    for part in range(PARTS):
        x_copy(mate, part, mate, 1).wait_recv()
    part_p[0] += project(mate, 0, 0, TOK)
    part_p[1] += project(mate, 1, 0, TOK)
    pass_on(0)
    own(2)
    pass_on(1)
    own(3)
    part_p[2] += project(mate, 2, 0, TOK)
    part_p[3] += project(mate, 3, 0, TOK)

    for chunk in range(4):
        half, pair = chunk // 2, chunk % 2
        if pair == 0:
            x_copy(diag, 2 * half, mate, 2).wait_recv()
            x_copy(diag, 2 * half + 1, mate, 2).wait_recv()
        if chunk == 0:
            pass_on(2)
        low, high = half * HALF, (half + 1) * HALF
        turned = []
        for k in (2 * pair, 2 * pair + 1):
            p = part_p[k, low:high, :] + project(across, k, low, high) + project(diag, k, low, high)
            turned.append(p.T.reshape(SEQ, SHARE, HALF))
        out_p[chunk] = jnp.concatenate(turned, axis=1).astype(jnp.bfloat16)
        if chunk == 0:
            pass_on(3)

        def send_p(to):
            pltpu.make_async_remote_copy(
                out_p.at[chunk, to], got.at[chunk, s], p_send.at[chunk], p_recv.at[chunk],
                device_id=(to, c), device_id_type=MESH,
            ).start()

        for_peers(s, c, send_p)
        got[chunk, pl.ds(s, 1)] = out_p[chunk, pl.ds(s, 1)]

    wait_bytes(flt.at[pl.ds(0, SEQ - 8)], g_recv)
    toeplitz(flt, table)

    for chunk in range(4):
        wait_bytes(got.at[chunk, pl.ds(0, SEQ - 1)], p_recv.at[chunk])
        load_blocks(got, chunk, even, odd)
        for group in range(SEQ // LAGS):
            conv_lags(table, even, odd, acc, chunk, group)
            if chunk == 3:
                y = acc[64 * group : 64 * (group + 1), :].reshape(LAGS, SHARE, TOK)
                y = jnp.concatenate([y[:, :, :HALF], y[:, :, HALF:]], axis=1)
                out_y[LAGS * group : LAGS * (group + 1)] = y.astype(jnp.bfloat16)

    def send_y(to):
        pltpu.make_async_remote_copy(
            out_y.at[to], got_y.at[s], y_send, y_recv, device_id=(to, c), device_id_type=MESH
        ).start()

    for_peers(s, c, send_y)
    got_y[pl.ds(s, 1)] = out_y[pl.ds(s, 1)]
    for part in range(PARTS):
        x_copy(c, part, across, 0).wait_send()
        x_copy(c, part, mate, 1).wait_send()
        x_copy(across, part, mate, 2).wait_send()
    wait_bytes(flt.at[pl.ds(0, 7)], f_send)
    wait_bytes(flt.at[pl.ds(0, SEQ - 8)], g_send)
    for k in range(K):
        wait_bytes(out_p.at[k, pl.ds(0, SEQ - 1)], p_send.at[k])

    wait_bytes(got_y.at[pl.ds(0, SEQ - 1)], y_recv)
    wait_bytes(out_y.at[pl.ds(0, SEQ - 1)], y_send)


def turn_back(y_ref, o_ref):
    r = y_ref[...].astype(jnp.float32)
    for half in range(2):
        block = r[:, half * SHARE : (half + 1) * SHARE, :].reshape(FEAT, HALF)
        o_ref[half * HALF : (half + 1) * HALF, :] = block.T.astype(jnp.bfloat16)


def local(inputs, weights, filters):
    bf16, f32 = jnp.bfloat16, jnp.float32
    vmem = pl.BlockSpec(memory_space=pltpu.VMEM)
    dma = pltpu.SemaphoreType.DMA
    y = pl.pallas_call(
        kernel,
        out_shape=jax.ShapeDtypeStruct((SEQ, 16, HALF), bf16),
        in_specs=[pl.BlockSpec(memory_space=pl.ANY)] * 3,
        out_specs=vmem,
        scratch_shapes=[
            pltpu.VMEM((CHAN, TOK, FEAT), bf16),
            pltpu.VMEM((K, CHAN * FEAT, FEAT), bf16),
            pltpu.VMEM((K, TOK), f32),
            pltpu.VMEM((SEQ, 8, HALF), f32),
            pltpu.VMEM((K, TOK, FEAT), f32),
            pltpu.VMEM((K, SEQ, 16, HALF), bf16),
            pltpu.VMEM((K, SEQ, 16, HALF), bf16),
            pltpu.VMEM((K, 2 * SEQ + 1, HALF, HALF), bf16),
            pltpu.VMEM((2, 576, HALF), bf16),
            pltpu.VMEM((2, 592, HALF), bf16),
            pltpu.VMEM((512, TOK), f32),
            pltpu.VMEM((SEQ, 16, HALF), bf16),
            dma((2,)),
            dma((K,)),
            dma((3, PARTS)),
            dma((3, PARTS)),
            dma,
            dma,
            dma,
            dma,
            dma((K,)),
            dma((K,)),
            dma,
            dma,
        ],
        compiler_params=pltpu.CompilerParams(
            collective_id=0, has_side_effects=True, vmem_limit_bytes=56 << 20
        ),
        cost_estimate=pl.CostEstimate(
            flops=11 * 10**9, bytes_accessed=10**7, transcendentals=0
        ),
    )(inputs, weights, filters)
    return pl.pallas_call(
        turn_back,
        out_shape=jax.ShapeDtypeStruct((TOK, FEAT), bf16),
        in_specs=[vmem],
        out_specs=vmem,
        cost_estimate=pl.CostEstimate(flops=0, bytes_accessed=2**19, transcendentals=0),
    )(y)


def solution(mesh):
    in_specs = (P("seq", "chan"), P(None, None, "chan"), P(None, "seq"))
    out_specs = P("seq", "chan")
    return jax.shard_map(local, mesh=mesh, in_specs=in_specs, out_specs=out_specs, check_vma=False)
```

```python
import functools

import jax
import jax.numpy as jnp
from jax import lax
from jax.experimental import pallas as pl
from jax.experimental.pallas import tpu as pltpu
from jax.sharding import PartitionSpec as P

MESH = pl.DeviceIdType.MESH
SEQ = 64
CHAN = 4
K = 4
TOK = 256
FEAT = 512
HALF = 128
SHARE = FEAT // SEQ
LAGS = 8
BLOCKS = 8
PARTS = 4


def peer(s, c, o):
    i, r = (SEQ - o) // 8, (SEQ - o) % 8
    h = (i + 1) // 2
    oz = h + (1 - i % 2) * (8 - 2 * h)
    oz = oz + (c % 2) * (8 - 2 * oz)
    yh, x, z = s // 32, (s // 8) % 4, s % 8
    return ((yh + r // 4) % 2) * 32 + ((x + r) % 4) * 8 + (z + oz) % 8


def wait_bytes(ref, sem):
    pltpu.make_async_copy(ref, ref, sem).wait()


def toeplitz(flt, table):
    row = lax.broadcasted_iota(jnp.int32, (16, HALF), 0)
    col = lax.broadcasted_iota(jnp.int32, (16, HALF), 1)

    def turned(line):
        wide = jnp.broadcast_to(line, (16, HALF))
        return pltpu.roll(wide, 0, axis=1, stride=1, stride_axis=0).astype(jnp.bfloat16)

    for k in range(K):
        table[k, 0] = jnp.zeros((HALF, HALF), jnp.bfloat16)

    def step(m0, carry):
        for k in range(K):
            last = flt[jnp.maximum(m0 * BLOCKS - 1, 0), pl.ds(K + k, 1), :]
            base = [turned(jnp.where(m0 == 0, 0.0, last))]
            for m in range(BLOCKS):
                for q in range(2):
                    base.append(turned(flt[m0 * BLOCKS + m, pl.ds(q * K + k, 1), :]))
            for i in range(HALF // 16):
                moved = base if i == 0 else [pltpu.roll(b, 16 * i, axis=1) for b in base]
                for n in range(2 * BLOCKS):
                    table[k, 2 * BLOCKS * m0 + n + 1, 16 * i : 16 * (i + 1), :] = jnp.where(
                        col >= row + 16 * i, moved[n + 1], moved[n]
                    )
        return carry

    lax.fori_loop(0, SEQ // BLOCKS, step, 0)


def load_blocks(got, chunk, even, odd):
    v = got[chunk].astype(jnp.float32)
    zero = jnp.zeros((SHARE, HALF), jnp.float32)
    for kk in range(2):
        a = v[:, kk * SHARE : (kk + 1) * SHARE, :].reshape(SEQ * SHARE, HALF)
        even[kk, 64:576, :] = a.astype(jnp.bfloat16)
        odd[kk, 64:592, :] = jnp.concatenate([zero, a, zero], axis=0).astype(jnp.bfloat16)


def conv_lags(table, even, odd, acc, chunk, group):
    half, pair = chunk // 2, chunk % 2
    low = 64 * group
    rows = 512 - low
    lhs, rhs = [], []
    for kk in range(2):
        for jj in range(LAGS):
            at = 64 - 8 * jj
            if jj % 2 == 0:
                lhs.append(even[kk, at : at + rows, :])
            else:
                lhs.append(odd[kk, at + 8 : at + 8 + rows, :])
            n = 2 * (LAGS * group + jj) + 1 - half
            k = 2 * pair + kk
            rhs.append(jnp.concatenate([table[k, n], table[k, n + 1]], axis=1))
    part = jnp.dot(
        jnp.concatenate(lhs, axis=1),
        jnp.concatenate(rhs, axis=0),
        preferred_element_type=jnp.float32,
    )
    if chunk == 0 and group == 0:
        acc[low:, :] = part
    else:
        acc[low:, :] += part


def kernel(
    x_hbm, w_hbm, f_hbm, got_y,
    xs, w, fsrc, flt, part_p, out_p, got, table, even, odd, acc, out_y,
    in_sem, w_sem, xs_send, xs_recv, f_send, f_recv, g_send, g_recv, p_send, p_recv, y_send, y_recv,
):
    s, c = lax.axis_index("seq"), lax.axis_index("chan")
    mate = c + 1 - 2 * (c % 2)
    across = (c + 2) % 4
    diag = (mate + 2) % 4

    bar = pltpu.get_barrier_semaphore()
    for i in range(1, CHAN):
        pl.semaphore_signal(bar, inc=1, device_id=(s, (c + i) % CHAN), device_id_type=MESH)

    @pl.loop(1, SEQ)
    def _(o):
        pl.semaphore_signal(bar, inc=1, device_id=((s + o) % SEQ, c), device_id_type=MESH)

    x_in = pltpu.make_async_copy(x_hbm, xs.at[c], in_sem.at[0])
    f_in = pltpu.make_async_copy(f_hbm, fsrc, in_sem.at[1])
    x_in.start()
    f_in.start()
    for k in range(K):
        pltpu.make_async_copy(w_hbm.at[k], w.at[k], w_sem.at[k]).start()
    for kk in range(2):
        even[kk, 0:64, :] = jnp.zeros((64, HALF), jnp.bfloat16)
        odd[kk, 0:64, :] = jnp.zeros((64, HALF), jnp.bfloat16)
    f_in.wait()
    f = fsrc[...]
    flt[pl.ds(s, 1)] = jnp.concatenate([f[:, :HALF], f[:, HALF:]], axis=0)[None]
    x_in.wait()
    pl.semaphore_wait(bar, SEQ - 1 + CHAN - 1)

    rows = TOK // PARTS

    def x_copy(owner, part, to, kind):
        at = xs.at[owner, pl.ds(part * rows, rows)]
        return pltpu.make_async_remote_copy(
            at, at, xs_send.at[kind, part], xs_recv.at[kind, part],
            device_id=(s, to), device_id_type=MESH,
        )

    for part in range(PARTS):
        x_copy(c, part, across, 0).start()
    for part in range(PARTS):
        x_copy(c, part, mate, 1).start()

    line, z = s // 8, s % 8

    def near_copy(i):
        return pltpu.make_async_remote_copy(
            flt.at[s], flt.at[s], f_send, f_recv,
            device_id=(line * 8 + (z + i) % 8, c), device_id_type=MESH,
        )

    def line_copy(i):
        block = flt.at[pl.ds(line * 8, 8)]
        return pltpu.make_async_remote_copy(
            block, block, g_send, g_recv,
            device_id=((line + i) % 8 * 8 + z, c), device_id_type=MESH,
        )

    for i in range(1, 8):
        near_copy(i).start()

    def pass_on(part):
        x_copy(across, part, across, 0).wait_recv()
        x_copy(across, part, mate, 2).start()

    def project(owner, k, low, high):
        return jnp.dot(
            xs[owner, low:high, :],
            w[k, pl.ds(pl.multiple_of(owner * FEAT, FEAT), FEAT), :],
            preferred_element_type=jnp.float32,
        )

    def own(k):
        pltpu.make_async_copy(w_hbm.at[k], w.at[k], w_sem.at[k]).wait()
        part_p[k] = project(c, k, 0, TOK)

    own(0)
    own(1)
    wait_bytes(flt.at[pl.ds(0, 7)], f_recv)
    for i in range(1, 8):
        line_copy(i).start()
    for part in range(PARTS):
        x_copy(mate, part, mate, 1).wait_recv()
    part_p[0] += project(mate, 0, 0, TOK)
    part_p[1] += project(mate, 1, 0, TOK)
    pass_on(0)
    own(2)
    pass_on(1)
    own(3)
    part_p[2] += project(mate, 2, 0, TOK)
    part_p[3] += project(mate, 3, 0, TOK)

    for chunk in range(4):
        half, pair = chunk // 2, chunk % 2
        if pair == 0:
            x_copy(diag, 2 * half, mate, 2).wait_recv()
            x_copy(diag, 2 * half + 1, mate, 2).wait_recv()
        if chunk == 0:
            pass_on(2)
        low, high = half * HALF, (half + 1) * HALF
        turned = []
        for k in (2 * pair, 2 * pair + 1):
            p = part_p[k, low:high, :] + project(across, k, low, high) + project(diag, k, low, high)
            turned.append(p.T.reshape(SEQ, SHARE, HALF))
        out_p[chunk] = jnp.concatenate(turned, axis=1).astype(jnp.bfloat16)
        if chunk == 0:
            pass_on(3)

        if chunk > 0:
            first, count = (0, 2) if chunk == 1 else (chunk, 1)

            @pl.loop(1, SEQ)
            def _(o):
                to = peer(s, c, o)
                pltpu.make_async_remote_copy(
                    out_p.at[pl.ds(first, count), to], got.at[pl.ds(first, count), s],
                    p_send.at[chunk], p_recv.at[chunk],
                    device_id=(to, c), device_id_type=MESH,
                ).start()

        got[chunk, pl.ds(s, 1)] = out_p[chunk, pl.ds(s, 1)]

    wait_bytes(flt.at[pl.ds(0, SEQ - 8)], g_recv)
    toeplitz(flt, table)

    for chunk in range(4):
        if chunk == 0:
            wait_bytes(got.at[pl.ds(0, 2), pl.ds(0, SEQ - 1)], p_recv.at[1])
        if chunk > 1:
            wait_bytes(got.at[chunk, pl.ds(0, SEQ - 1)], p_recv.at[chunk])
        load_blocks(got, chunk, even, odd)
        for group in range(SEQ // LAGS):
            conv_lags(table, even, odd, acc, chunk, group)
            if chunk == 3:
                y = acc[64 * group : 64 * (group + 1), :].reshape(LAGS, SHARE, TOK)
                y = jnp.concatenate([y[:, :, :HALF], y[:, :, HALF:]], axis=1)
                out_y[LAGS * group : LAGS * (group + 1)] = y.astype(jnp.bfloat16)

    @pl.loop(1, SEQ)
    def _(o):
        to = peer(s, c, o)
        pltpu.make_async_remote_copy(
            out_y.at[to], got_y.at[s], y_send, y_recv, device_id=(to, c), device_id_type=MESH
        ).start()

    got_y[pl.ds(s, 1)] = out_y[pl.ds(s, 1)]
    for part in range(PARTS):
        x_copy(c, part, across, 0).wait_send()
        x_copy(c, part, mate, 1).wait_send()
        x_copy(across, part, mate, 2).wait_send()
    wait_bytes(flt.at[pl.ds(0, 7)], f_send)
    wait_bytes(flt.at[pl.ds(0, SEQ - 8)], g_send)
    wait_bytes(out_p.at[pl.ds(0, 2), pl.ds(0, SEQ - 1)], p_send.at[1])
    for k in range(2, K):
        wait_bytes(out_p.at[k, pl.ds(0, SEQ - 1)], p_send.at[k])

    wait_bytes(got_y.at[pl.ds(0, SEQ - 1)], y_recv)
    wait_bytes(out_y.at[pl.ds(0, SEQ - 1)], y_send)


def turn_back(y_ref, o_ref):
    r = y_ref[...].astype(jnp.float32)
    for half in range(2):
        block = r[:, half * SHARE : (half + 1) * SHARE, :].reshape(FEAT, HALF)
        o_ref[half * HALF : (half + 1) * HALF, :] = block.T.astype(jnp.bfloat16)


def local(inputs, weights, filters):
    bf16, f32 = jnp.bfloat16, jnp.float32
    vmem = pl.BlockSpec(memory_space=pltpu.VMEM)
    dma = pltpu.SemaphoreType.DMA
    y = pl.pallas_call(
        kernel,
        out_shape=jax.ShapeDtypeStruct((SEQ, 16, HALF), bf16),
        in_specs=[pl.BlockSpec(memory_space=pl.ANY)] * 3,
        out_specs=vmem,
        scratch_shapes=[
            pltpu.VMEM((CHAN, TOK, FEAT), bf16),
            pltpu.VMEM((K, CHAN * FEAT, FEAT), bf16),
            pltpu.VMEM((K, TOK), f32),
            pltpu.VMEM((SEQ, 8, HALF), f32),
            pltpu.VMEM((K, TOK, FEAT), f32),
            pltpu.VMEM((K, SEQ, 16, HALF), bf16),
            pltpu.VMEM((K, SEQ, 16, HALF), bf16),
            pltpu.VMEM((K, 2 * SEQ + 1, HALF, HALF), bf16),
            pltpu.VMEM((2, 576, HALF), bf16),
            pltpu.VMEM((2, 592, HALF), bf16),
            pltpu.VMEM((512, TOK), f32),
            pltpu.VMEM((SEQ, 16, HALF), bf16),
            dma((2,)),
            dma((K,)),
            dma((3, PARTS)),
            dma((3, PARTS)),
            dma,
            dma,
            dma,
            dma,
            dma((K,)),
            dma((K,)),
            dma,
            dma,
        ],
        compiler_params=pltpu.CompilerParams(
            collective_id=0, has_side_effects=True, vmem_limit_bytes=56 << 20
        ),
        cost_estimate=pl.CostEstimate(
            flops=11 * 10**9, bytes_accessed=10**7, transcendentals=0
        ),
    )(inputs, weights, filters)
    return pl.pallas_call(
        turn_back,
        out_shape=jax.ShapeDtypeStruct((TOK, FEAT), bf16),
        in_specs=[vmem],
        out_specs=vmem,
        cost_estimate=pl.CostEstimate(flops=0, bytes_accessed=2**19, transcendentals=0),
    )(y)


def solution(mesh):
    in_specs = (P("seq", "chan"), P(None, None, "chan"), P(None, "seq"))
    out_specs = P("seq", "chan")
    return jax.shard_map(local, mesh=mesh, in_specs=in_specs, out_specs=out_specs, check_vma=False)
```
